512 devices in a mesh: seq: 16 (over y, core), head: 32 (over z, x).
Axes of the slice: x: 4, y: 8, z: 8, core: 2. Of those that a mesh axis runs over, the one named last changes fastest.
Arguments:
- queries: bfloat16 [65536, 8192], P(('seq', 'head')), may hold values from -36 to 36
- keys_values: bfloat16 [65536, 2048], P(('seq', 'head')), may hold values from -14 to 14
- vertical: int32 [64, 4], replicated, may hold values from -1 to 63, as said below
- slash: int32 [64, 2], replicated, may hold values from -1 to 2, as said below
- assignment: int32 [64], replicated, may hold values from 0 to 63, as said below
Outputs:
- attended: bfloat16 [1024, 4096, 128], P(('seq', 'head'))
The draws below stay inside these ranges and needn't reach their ends.
Inputs may be any that keep to these rules, and one draw needn't show every extreme that they name: `vertical`: row h lists distinct blocks below 64, used entries first and -1 after them; a row uses 1 to 4 entries. The rows of the 8 query heads of one key-value head name exactly 8 distinct blocks together. `slash`: row h lists distinct offsets, used entries first and -1 after them; a row uses 1 to 2 entries. `assignment`: every unit appears once. Slots 2 * d to 2 * d + 1 of a group belong to index d of the head axis, and their units are parts of query heads of one key-value head.
All inputs are finite; a program needn't handle non-finite values.
Results may differ from the reference program's by a relative error of at most 0.0065.
Values may be sent and summed in bfloat16 or wider, within the bound.
A program may use at most 64 MiB of HBM per device.

```python
import math
import jax
import jax.numpy as jnp
from jax import lax

HQ = 64
HK = 8
HD = 128
BLK = 64
REACH = 2
NS = 2
NV = 4
GQ = 8
VPOOL = 8
SPLITS = 1
UNITS = 64
SLOTS = 2
PORTION = 128
UROWS = 4096
TOKENS = 65536
VREG = 64
N_SEQ = 16
N_HEAD = 32


def pattern(key):
    pool_key = jax.random.fold_in(key, 11)
    rank_key = jax.random.fold_in(key, 12)
    count_key = jax.random.fold_in(key, 13)
    pick_key = jax.random.fold_in(key, 14)
    offset_key = jax.random.fold_in(key, 15)
    many_key = jax.random.fold_in(key, 16)
    order_key = jax.random.fold_in(key, 17)
    device_key = jax.random.fold_in(key, 18)
    chosen_key = jax.random.fold_in(key, 19)
    other_key = jax.random.fold_in(key, 20)
    region = jnp.arange(VREG, dtype=jnp.int32)
    pool_scores = jax.random.randint(pool_key, (HK, VREG), 0, 1 << 16, dtype=jnp.int32) * VREG + region[None, :]
    pool_scores = jnp.where((jnp.arange(HK)[:, None] == 0) & (region[None, :] == VREG - 1), 1 << 30, pool_scores)
    pools = lax.top_k(pool_scores, VPOOL)[1].astype(jnp.int32)
    local = jnp.arange(GQ, dtype=jnp.int32)
    rank_scores = jax.random.randint(rank_key, (HK, GQ), 0, 1 << 16, dtype=jnp.int32) * GQ + local[None, :]
    ranks = jnp.argsort(jnp.argsort(-rank_scores, axis=1), axis=1).reshape(HQ).astype(jnp.int32)
    owners = jnp.arange(HQ, dtype=jnp.int32) // GQ
    counts = jax.random.randint(count_key, (HQ,), 1, NV + 1, dtype=jnp.int32)
    counts = jnp.where(ranks < 2, NV, counts)
    counts = jnp.where((owners == 0) & (ranks == 2), 1, counts)
    pick_scores = jax.random.randint(pick_key, (HQ, VPOOL), 0, 1 << 16, dtype=jnp.int32) * VPOOL + jnp.arange(VPOOL, dtype=jnp.int32)[None, :]
    picks = lax.top_k(pick_scores, NV)[1].astype(jnp.int32)
    own_pool = pools[owners]
    chosen = jnp.take_along_axis(own_pool, picks, axis=1)
    lower = own_pool[:, :NV]
    upper = own_pool[:, NV:]
    lists = jnp.where((ranks == 0)[:, None], lower, jnp.where((ranks == 1)[:, None], upper, chosen))
    vertical = jnp.where(jnp.arange(NV, dtype=jnp.int32)[None, :] < counts[:, None], lists, -1).astype(jnp.int32)
    heads = jnp.arange(HQ, dtype=jnp.int32)
    full_head = jax.random.randint(chosen_key, (), 0, HQ, dtype=jnp.int32)
    single_head = (full_head + 1 + jax.random.randint(other_key, (), 0, HQ - 1, dtype=jnp.int32)) % HQ
    reach_index = jnp.arange(REACH, dtype=jnp.int32)
    reach_scores = jax.random.randint(offset_key, (HQ, REACH), 0, 1 << 16, dtype=jnp.int32) * REACH + reach_index[None, :]
    reach_scores = jnp.where((heads[:, None] == full_head) & (reach_index[None, :] == REACH - 1), 1 << 30, reach_scores)
    offsets = lax.top_k(reach_scores, NS)[1].astype(jnp.int32) + 1
    many = jax.random.randint(many_key, (HQ,), 1, NS + 1, dtype=jnp.int32)
    many = jnp.where(heads == full_head, NS, jnp.where(heads == single_head, 1, many))
    slash = jnp.where(jnp.arange(NS, dtype=jnp.int32)[None, :] < many[:, None], offsets, -1).astype(jnp.int32)
    cost = 1 + many + counts
    members_total = SPLITS * GQ
    index = jnp.arange(members_total, dtype=jnp.int32)
    units = index[None, :] // GQ * HQ + jnp.arange(HK, dtype=jnp.int32)[:, None] * GQ + index[None, :] % GQ
    unit_cost = cost[units % HQ]
    order_scores = unit_cost * (1 << 20) + jax.random.randint(order_key, (HK, members_total), 0, 1 << 8, dtype=jnp.int32) * members_total + index[None, :]
    ranked = jnp.take_along_axis(units, jnp.argsort(-order_scores, axis=1), axis=1)
    columns = members_total // SLOTS
    grid = ranked.reshape(HK, SLOTS, columns)
    odd = (jnp.arange(SLOTS, dtype=jnp.int32) % 2 == 1)[None, :, None]
    snaked = jnp.where(odd, grid[:, :, ::-1], grid)
    groups = jnp.transpose(snaked, (0, 2, 1)).reshape(HK * columns, SLOTS)
    shuffle = jax.random.permutation(device_key, HK * columns)
    assignment = groups[shuffle].reshape(UNITS).astype(jnp.int32)
    return (vertical, slash, assignment)


def draw_keys(key):
    key_part = jax.random.fold_in(key, 101)
    keys = jnp.clip(jax.random.normal(key_part, (TOKENS, HK, HD), jnp.float32), -4.5, 4.5)
    return keys


def draw_queries(key, part):
    query_part = jax.random.fold_in(key, 103)
    queries = jnp.clip(jax.random.normal(query_part, (TOKENS, HQ, HD), jnp.float32) * 1.5, -9.0, 9.0)
    return queries.reshape(TOKENS, HQ * HD).astype(jnp.bfloat16)


def draw_keys_values(key, part):
    value_part = jax.random.fold_in(key, 102)
    keys = draw_keys(key)
    values = jnp.clip(jax.random.normal(value_part, (TOKENS, HK, HD), jnp.float32) * 3.0, -13.5, 13.5)
    pairs = jnp.stack([keys, values], axis=2).reshape(TOKENS, 2 * HK * HD)
    return pairs.astype(jnp.bfloat16)


def draw_vertical(key, part):
    return pattern(key)[0]


def draw_slash(key, part):
    return pattern(key)[1]


def draw_assignment(key, part):
    return pattern(key)[2]


def setup_inputs(seed: int = 0) -> dict:
    key_list = jax.random.split(jax.random.key(seed), 6)
    return {
        "queries": draw_queries(jax.random.fold_in(key_list[5], 71), 0),
        "keys_values": draw_keys_values(jax.random.fold_in(key_list[5], 71), 0),
        "vertical": draw_vertical(jax.random.fold_in(key_list[5], 71), 0),
        "slash": draw_slash(jax.random.fold_in(key_list[5], 71), 0),
        "assignment": draw_assignment(jax.random.fold_in(key_list[5], 71), 0),
    }


def reference(queries, keys_values, vertical, slash, assignment):
    total_blocks = TOKENS // BLK
    span = 32
    spans = total_blocks // span
    slots = 1 + NS + NV
    query_heads = jnp.transpose(queries.reshape(total_blocks, BLK, HQ, HD), (2, 0, 1, 3))
    pair_heads = jnp.transpose(keys_values.reshape(total_blocks, BLK, HK, 2 * HD), (2, 0, 1, 3))
    scale = 1.0 / math.sqrt(HD)
    causal = jnp.arange(BLK)[None, :] <= jnp.arange(BLK)[:, None]
    slot_kind = (jnp.arange(slots)[None, :, None] > 0) | causal[:, None, :]

    def one_item(item):
        head = (item // spans).astype(jnp.int32)
        first = (item % spans * span).astype(jnp.int32)
        owner = (head // GQ).astype(jnp.int32)
        query_index = first + jnp.arange(span, dtype=jnp.int32)
        zero = jnp.zeros((), jnp.int32)
        block_queries = lax.dynamic_slice(query_heads, (head, first, zero, zero), (1, span, BLK, HD))[0].astype(jnp.float32)
        vertical_row = vertical[head]
        slash_row = slash[head]
        slash_blocks = query_index[:, None] - slash_row[None, :]
        repeated = jnp.any(slash_blocks[:, :, None] == vertical_row[None, None, :], axis=-1)
        slash_valid = (slash_row[None, :] >= 1) & (slash_blocks >= 0) & jnp.logical_not(repeated)
        vertical_blocks = jnp.broadcast_to(vertical_row[None, :], (span, NV))
        vertical_valid = (vertical_blocks >= 0) & (vertical_blocks < query_index[:, None])
        blocks = jnp.concatenate([query_index[:, None], slash_blocks, vertical_blocks], axis=1)
        valid = jnp.concatenate([jnp.ones((span, 1), jnp.bool_), slash_valid, vertical_valid], axis=1)
        fetched = pair_heads[owner, jnp.clip(blocks, 0, total_blocks - 1)].astype(jnp.float32)
        keys = fetched[..., :HD]
        values = fetched[..., HD:]
        scores = jnp.einsum('nqd,nskd->nqsk', block_queries, keys) * scale
        mask = valid[:, None, :, None] & slot_kind[None]
        masked = jnp.where(mask, scores, -jnp.inf)
        top = lax.optimization_barrier(jnp.max(masked, axis=(2, 3), keepdims=True))
        weights = jnp.where(mask, jnp.exp(scores - top), 0.0)
        total = lax.optimization_barrier(jnp.sum(weights, axis=(2, 3)))
        rounded = lax.optimization_barrier(weights.astype(jnp.bfloat16)).astype(jnp.float32)
        numer = jnp.einsum('nqsk,nskd->nqd', rounded, values)
        return (numer / total[..., None]).astype(jnp.bfloat16)
    results = lax.map(one_item, jnp.arange(HQ * spans, dtype=jnp.int32))
    attention = results.reshape(HQ, N_SEQ, N_HEAD, SPLITS, PORTION, HD)
    picked = attention[assignment % HQ, :, :, assignment // HQ]
    return jnp.transpose(picked, (1, 0, 2, 3, 4)).reshape(N_SEQ * UNITS, UROWS, HD)
```

```python
import functools
import math

import jax
import jax.numpy as jnp
from jax import lax
from jax.experimental import pallas as pl
from jax.experimental.pallas import tpu as pltpu
from jax.sharding import PartitionSpec as P

HD = 128
BLK = 64
NV = 4
NX = 4
CH = 16
NC = BLK // CH
ROWS = 2 * BLK
VPOOL = 8
HIDE = -1e30
MESH = pl.DeviceIdType.MESH


def table_kernel(group, vert_ref, assign_ref, out_ref):
    v = vert_ref[...]
    heads = v.shape[0]
    block = lax.broadcasted_iota(jnp.int32, (heads, BLK), 1)
    used = jnp.zeros((heads, BLK), jnp.float32)
    for n in range(NV):
        used = jnp.maximum(used, (v[:, n : n + 1] == block).astype(jnp.float32))
    one = lax.broadcasted_iota(jnp.int32, (heads, heads), 0)
    other = lax.broadcasted_iota(jnp.int32, (heads, heads), 1)
    same = (one // group == other // group).astype(jnp.float32)
    some = jnp.dot(same, used, preferred_element_type=jnp.float32)
    pool = (some > 0.5).astype(jnp.float32)
    before = (
        lax.broadcasted_iota(jnp.int32, (BLK, BLK), 0)
        < lax.broadcasted_iota(jnp.int32, (BLK, BLK), 1)
    ).astype(jnp.float32)
    rank = jnp.dot(pool, before, preferred_element_type=jnp.float32)
    lane = lax.broadcasted_iota(jnp.int32, (heads, HD), 1)
    table = jnp.zeros((heads, HD), jnp.float32)
    for n in range(NV):
        place = jnp.sum(jnp.where(v[:, n : n + 1] == block, rank, 0.0), axis=1, keepdims=True)
        table = jnp.where(lane == n, place, table)
    number = block.astype(jnp.float32)
    for r in range(VPOOL):
        held = (pool > 0.5) & (rank > r - 0.5) & (rank < r + 0.5)
        place = jnp.sum(jnp.where(held, number, 0.0), axis=1, keepdims=True)
        table = jnp.where(lane == 8 + r, place, table)
    head = lax.broadcasted_iota(jnp.int32, (heads, HD), 0)
    table = jnp.where(lane == 4, head.astype(jnp.float32), table)
    table = jnp.where(lane == 5, (head // group).astype(jnp.float32), table)
    chosen = (assign_ref[...] % heads == other).astype(jnp.float32)
    out_ref[:heads] = table.astype(jnp.int32)
    slots = jnp.dot(chosen, table, preferred_element_type=jnp.float32)
    out_ref[heads:] = slots.astype(jnp.int32)


def main_kernel(
    sizes,
    table,
    vert_ref,
    slash_ref,
    q_hbm,
    kv_hbm,
    out,
    q_v,
    kcat,
    tbuf,
    piece,
    pool,
    stage,
    rows_bias,
    causal_bias,
    sems,
    bar_free,
):
    NS, NH, NZ, NY, HQ, HK = sizes
    GQ = HQ // HK
    owners = 2 * HK * NC
    seq = lax.axis_index("seq")
    head = lax.axis_index("head")
    y, core = seq // 2, seq % 2
    z, x = head // NX, head % NX
    a = y + core * (z - y)
    b = z + core * (y - z)

    def device(core_, a_, b_, x_):
        y_ = a_ + core_ * (b_ - a_)
        z_ = b_ + core_ * (a_ - b_)
        return y_ * 2 + core_, z_ * NX + x_

    def home(a_, c_):
        return (a_ + 2 * c_) % NZ

    owner = b == home(a, x)
    source = seq == 0
    one = jnp.int32(1)
    nil = jnp.int32(0)
    own_source = jnp.where(owner & source, one, nil)

    def columns(n):
        return pl.ds(pl.multiple_of(n * HD, HD), HD)

    @pl.loop(0, HQ)
    def _(n):
        pltpu.make_async_copy(q_hbm.at[:, columns(n)], q_v.at[n], sems.at[0]).start()

    @pl.loop(0, 2 * HK)
    def _(n):
        pltpu.make_async_copy(kv_hbm.at[:, :, :, columns(n)], kcat.at[n, 1], sems.at[1]).start()

    barrier = pltpu.get_barrier_semaphore()

    def greet(s_, h_):
        pl.semaphore_signal(barrier, inc=1, device_id=(s_, h_), device_id_type=MESH)

    @pl.when(owner)
    def _():
        @pl.loop(0, NH)
        def _(s):
            @pl.when(jnp.logical_not(source & (head == s)))
            def _():
                greet(0, s)

    @pl.loop(1, NH)
    def _(k):
        greet(seq, (head + k) % NH)

    @pl.loop(1, NY)
    def _(k):
        other = (y + k) % NY * 2 + core
        greet(other, head)

        @pl.when(core == 1)
        def _():
            for dx in range(1, NX):
                greet(other, z * NX + (x + dx) % NX)

    greet(y * 2 + 1 - core, head)

    @pl.when((head == 0) & (seq > 0))
    def _():
        greet(seq - 1, NH - 1)

    base = (seq * NH + head) * 2
    vert = vert_ref[...]
    slash = slash_ref[...]
    lane = lax.broadcasted_iota(jnp.int32, (HQ, 8 * BLK), 1) // BLK
    target = base + lane - 2
    listed = jnp.full((HQ, 8 * BLK), -1, jnp.int32)
    fresh = (target >= 0) & (lane < 4)
    for n in range(NV):
        col = vert[:, n : n + 1]
        listed = jnp.where(lane == 4 + n, col, listed)
        fresh = fresh & (target != col)
    for qb in range(2):
        off = qb + 2 - lane
        hit = (off >= 1) & ((slash[:, 0:1] == off) | (slash[:, 1:2] == off)) & fresh
        near = (lane < 4) & ((off == 0) | hit)
        far = (lane >= 4) & (listed >= 0) & (listed < base + qb)
        rows_bias[qb, :, 0] = jnp.where(near | far, 0.0, HIDE)
    row = lax.broadcasted_iota(jnp.int32, (ROWS, 2 * ROWS), 0)
    col = lax.broadcasted_iota(jnp.int32, (ROWS, 2 * ROWS), 1) - ROWS
    causal_bias[...] = jnp.where(col <= row, 0.0, HIDE)

    count = (NH - 1) + (NY - 1) * (1 + (NX - 1) * core) + 1
    count = count + jnp.where((head == NH - 1) & (seq < NS - 1), one, nil)
    count = count + jnp.where(source, owners - own_source, nil)
    pl.semaphore_wait(barrier, count)

    def remote(src, dst, send, recv, to):
        return pltpu.make_async_remote_copy(
            src_ref=src,
            dst_ref=dst,
            send_sem=sems.at[send],
            recv_sem=sems.at[recv],
            device_id=to,
            device_id_type=MESH,
        )

    def await_bytes(ref, sem):
        pltpu.make_async_copy(ref, ref, sems.at[sem]).wait()

    @pl.when(source)
    def _():
        @pl.loop(0, owners)
        def _(o):
            core_, a_, c_ = o // (HK * NC), o // NC % HK, o % NC
            s_, h_ = device(core_, a_, home(a_, c_), c_)
            src = kv_hbm.at[:, c_, :, columns(2 * a_ + core_)]
            dst = tbuf.at[pl.ds(2 * head, 2)]
            mine = (s_ == seq) & (h_ == head)

            @pl.when(mine)
            def _():
                pltpu.make_async_copy(src, dst, sems.at[3]).start()

            @pl.when(jnp.logical_not(mine))
            def _():
                remote(src, dst, 2, 3, (s_, h_)).start()

    last = (seq == NS - 1) & (head == NH - 1)
    first = (seq == 0) & (head == 0)
    wrap = jnp.where(head == NH - 1, one, nil)

    @pl.when(jnp.logical_not(last))
    def _():
        @pl.loop(0, 2 * HK)
        def _(n):
            src = kv_hbm.at[:, :, :, columns(n)]
            remote(src, kcat.at[n, 0], 4, 5, (seq + wrap, (head + 1) % NH)).start()

    @pl.when(first)
    def _():
        kcat[:, 0] = jnp.zeros((2 * HK, *kcat.shape[2:]), kcat.dtype)

    @pl.when(owner)
    def _():
        await_bytes(tbuf, 3)
        for r in range(VPOOL):
            piece[r] = tbuf[table[a * GQ, 8 + r]]

        @pl.loop(0, NZ * NX)
        def _(k):
            b_, x_ = k // NX, k % NX
            mine = (b_ == b) & (x_ == x)
            dst = pool.at[core, a, :, x]

            @pl.when(mine)
            def _():
                pltpu.make_async_copy(piece, dst, sems.at[7]).start()

            @pl.when(jnp.logical_not(mine))
            def _():
                remote(piece, dst, 6, 7, device(core, a, b_, x_)).start()

    await_bytes(pool.at[core, a], 7)

    @pl.loop(1, NY)
    def _(k):
        remote(pool.at[core, a], pool.at[core, a], 8, 9, device(core, (a + k) % NY, b, x)).start()

    await_bytes(pool.at[core, pl.ds(0, NY - 1)], 9)
    swap = remote(pool.at[core], pool.at[core], 10, 11, (y * 2 + 1 - core, head))
    swap.start()
    await_bytes(q_v, 0)
    await_bytes(kcat.at[:, 1], 1)

    @pl.when(jnp.logical_not(first))
    def _():
        await_bytes(kcat.at[:, 0], 5)

    await_bytes(pool.at[1 - core], 11)

    factor = math.log2(math.e) / math.sqrt(HD)
    contract = (((1,), (1,)), ((), ()))

    def attend(slot):
        h = table[HQ + slot, 4]
        c = table[HQ + slot, 5]
        query = q_v[h]
        keys = kcat[2 * c].reshape(2 * ROWS, HD)
        values = kcat[2 * c + 1].reshape(2 * ROWS, HD)
        places = [table[HQ + slot, n] for n in range(NV)]
        far_keys = jnp.concatenate([pool[0, c, p].reshape(BLK, HD) for p in places], axis=0)
        far_values = jnp.concatenate([pool[1, c, p].reshape(BLK, HD) for p in places], axis=0)
        bias = jnp.concatenate(
            [jnp.broadcast_to(rows_bias[qb, h], (BLK, 8 * BLK)) for qb in range(2)],
            axis=0,
        )
        near = lax.dot_general(query, keys, contract, preferred_element_type=jnp.float32)
        far = lax.dot_general(query, far_keys, contract, preferred_element_type=jnp.float32)
        near = near * factor + (bias[:, : 2 * ROWS] + causal_bias[...])
        far = far * factor + bias[:, 2 * ROWS :]
        top = jnp.maximum(
            jnp.max(near, axis=1, keepdims=True), jnp.max(far, axis=1, keepdims=True)
        )
        near = jnp.exp2(near - top)
        far = jnp.exp2(far - top)
        total = jnp.sum(near, axis=1, keepdims=True) + jnp.sum(far, axis=1, keepdims=True)
        numer = jnp.dot(
            near.astype(jnp.bfloat16), values, preferred_element_type=jnp.float32
        ) + jnp.dot(far.astype(jnp.bfloat16), far_values, preferred_element_type=jnp.float32)
        stage[slot] = (numer / total).astype(jnp.bfloat16)

    here = pl.ds(pl.multiple_of(head * ROWS, ROWS), ROWS)

    @pl.loop(1, NH + 1)
    def _(k):
        d = (head + k) % NH
        attend(2 * d)
        attend(2 * d + 1)
        src = stage.at[pl.ds(2 * d, 2)]
        dst = out.at[:, here]

        @pl.when(k == NH)
        def _():
            pltpu.make_async_copy(src, dst, sems.at[13]).start()

        @pl.when(k < NH)
        def _():
            remote(src, dst, 12, 13, (seq, d)).start()

    await_bytes(out, 13)
    await_bytes(stage.at[pl.ds(0, 2 * NH - 2)], 12)
    await_bytes(pool.at[core], 10)
    await_bytes(pool.at[core, pl.ds(0, NY - 1)], 8)

    @pl.when(owner)
    def _():
        await_bytes(stage.at[pl.ds(0, NZ * NX - 1)], 6)

    @pl.when(jnp.logical_not(last))
    def _():
        await_bytes(kv_hbm, 4)

    @pl.when(source & owner)
    def _():
        await_bytes(stage.at[pl.ds(0, owners - 1), pl.ds(0, 32)], 2)

    @pl.when(source & jnp.logical_not(owner))
    def _():
        await_bytes(stage.at[pl.ds(0, owners), pl.ds(0, 32)], 2)


def on_device(sizes, queries, keys_values, vertical, slash, assignment):
    NS, NH, NZ, NY, HQ, HK = sizes
    width = keys_values.shape[1]
    vmem = pl.BlockSpec(memory_space=pltpu.VMEM)
    smem = pl.BlockSpec(memory_space=pltpu.SMEM)
    hbm = pl.BlockSpec(memory_space=pl.ANY)
    table = pl.pallas_call(
        functools.partial(table_kernel, HQ // HK),
        out_shape=jax.ShapeDtypeStruct((2 * HQ, HD), jnp.int32),
        in_specs=[vmem, vmem],
        out_specs=vmem,
    )(vertical, assignment.reshape(HQ, 1))
    return pl.pallas_call(
        functools.partial(main_kernel, sizes),
        out_shape=jax.ShapeDtypeStruct((2, NH * ROWS, HD), jnp.bfloat16),
        in_specs=[smem, vmem, vmem, hbm, hbm],
        out_specs=hbm,
        scratch_shapes=[
            pltpu.VMEM((HQ, ROWS, HD), jnp.bfloat16),
            pltpu.VMEM((2 * HK, 2, 2, NC, CH, HD), jnp.bfloat16),
            pltpu.VMEM((2 * NH, CH, HD), jnp.bfloat16),
            pltpu.VMEM((VPOOL, CH, HD), jnp.bfloat16),
            pltpu.VMEM((2, HK, VPOOL, NC, CH, HD), jnp.bfloat16),
            pltpu.VMEM((max(2 * NH, 2 * HK * NC), ROWS, HD), jnp.bfloat16),
            pltpu.VMEM((2, HQ, 1, 8 * BLK), jnp.float32),
            pltpu.VMEM((ROWS, 2 * ROWS), jnp.float32),
            pltpu.SemaphoreType.DMA((14,)),
            pltpu.SemaphoreType.REGULAR,
        ],
        compiler_params=pltpu.CompilerParams(
            collective_id=0, has_side_effects=True, vmem_limit_bytes=40 * 2**20
        ),
    )(table, vertical, slash, queries, keys_values.reshape(2, NC, CH, width))


def solution(mesh):
    NS, NH = mesh.shape["seq"], mesh.shape["head"]
    sizes = (NS, NH, NH // NX, NS // 2, 2 * NH, NS // 2)
    placed = (P(("seq", "head"), None), P(("seq", "head"), None), P(), P(), P())
    return jax.shard_map(
        functools.partial(on_device, sizes),
        mesh=mesh,
        in_specs=placed,
        out_specs=P(("seq", "head"), None, None),
        check_vma=False,
    )
```

```python
import functools
import math

import jax
import jax.numpy as jnp
from jax import lax
from jax.experimental import pallas as pl
from jax.experimental.pallas import tpu as pltpu
from jax.sharding import PartitionSpec as P

HD = 128
BLK = 64
NV = 4
NX = 4
CH = 16
NC = BLK // CH
ROWS = 2 * BLK
VPOOL = 8
HIDE = -1e30
MESH = pl.DeviceIdType.MESH


def turned(rows):
    m = rows.shape[1]
    eye = (
        lax.broadcasted_iota(jnp.int32, (m, m), 0) == lax.broadcasted_iota(jnp.int32, (m, m), 1)
    ).astype(jnp.float32)
    return lax.dot_general(
        eye,
        rows.astype(jnp.float32),
        (((1,), (1,)), ((), ())),
        preferred_element_type=jnp.float32,
    ).astype(jnp.int32)


def fill_table(group, v, assign, out_ref):
    heads = v.shape[0]
    block = lax.broadcasted_iota(jnp.int32, (heads, BLK), 1)
    used = jnp.zeros((heads, BLK), jnp.float32)
    for n in range(NV):
        used = jnp.maximum(used, (v[:, n : n + 1] == block).astype(jnp.float32))
    one = lax.broadcasted_iota(jnp.int32, (heads, heads), 0)
    other = lax.broadcasted_iota(jnp.int32, (heads, heads), 1)
    same = (one // group == other // group).astype(jnp.float32)
    some = jnp.dot(same, used, preferred_element_type=jnp.float32)
    pool = (some > 0.5).astype(jnp.float32)
    before = (
        lax.broadcasted_iota(jnp.int32, (BLK, BLK), 0)
        < lax.broadcasted_iota(jnp.int32, (BLK, BLK), 1)
    ).astype(jnp.float32)
    rank = jnp.dot(pool, before, preferred_element_type=jnp.float32)
    lane = lax.broadcasted_iota(jnp.int32, (heads, HD), 1)
    table = jnp.zeros((heads, HD), jnp.float32)
    for n in range(NV):
        place = jnp.sum(jnp.where(v[:, n : n + 1] == block, rank, 0.0), axis=1, keepdims=True)
        table = jnp.where(lane == n, place, table)
    number = block.astype(jnp.float32)
    for r in range(VPOOL):
        held = (pool > 0.5) & (rank > r - 0.5) & (rank < r + 0.5)
        place = jnp.sum(jnp.where(held, number, 0.0), axis=1, keepdims=True)
        table = jnp.where(lane == 8 + r, place, table)
    head = lax.broadcasted_iota(jnp.int32, (heads, HD), 0)
    table = jnp.where(lane == 4, head.astype(jnp.float32), table)
    table = jnp.where(lane == 5, (head // group).astype(jnp.float32), table)
    chosen = (assign % heads == other).astype(jnp.float32)
    out_ref[:heads] = table.astype(jnp.int32)
    slots = jnp.dot(chosen, table, preferred_element_type=jnp.float32)
    out_ref[heads:] = slots.astype(jnp.int32)


def main_kernel(
    sizes,
    vert_ref,
    slash_ref,
    assign_ref,
    q_hbm,
    kv_hbm,
    out,
    q_v,
    kcat,
    tbuf,
    piece,
    pool,
    stage,
    rows_bias,
    causal_bias,
    table_v,
    table,
    sems,
    here_sem,
):
    NS, NH, NZ, NY, HQ, HK = sizes
    GQ = HQ // HK
    owners = 2 * HK * NC
    seq = lax.axis_index("seq")
    head = lax.axis_index("head")
    y, core = seq // 2, seq % 2
    z, x = head // NX, head % NX
    a = y + core * (z - y)
    b = z + core * (y - z)

    def device(core_, a_, b_, x_):
        y_ = a_ + core_ * (b_ - a_)
        z_ = b_ + core_ * (a_ - b_)
        return y_ * 2 + core_, z_ * NX + x_

    def home(a_, c_):
        return (a_ + 2 * c_) % NZ

    owner = b == home(a, x)
    source = seq == 0
    last = (seq == NS - 1) & (head == NH - 1)
    first = (seq == 0) & (head == 0)
    one = jnp.int32(1)
    nil = jnp.int32(0)
    own_source = jnp.where(owner & source, one, nil)

    def columns(n):
        return pl.ds(pl.multiple_of(n * HD, HD), HD)

    barrier = pltpu.get_barrier_semaphore()

    def greet(s_, h_):
        pl.semaphore_signal(barrier, inc=1, device_id=(s_, h_), device_id_type=MESH)

    @pl.when(owner)
    def _():
        @pl.loop(0, NH)
        def _(s):
            @pl.when(jnp.logical_not(source & (head == s)))
            def _():
                greet(0, s)

    @pl.loop(1, NZ)
    def _(k):
        greet(seq, (z + k) % NZ * NX + x)

    @pl.loop(1, NY)
    def _(k):
        greet((y + k) % NY * 2 + core, head)

    for k in range(1, NX):
        greet(seq, z * NX + (x + k) % NX)

    greet(y * 2 + 1 - core, head)

    @pl.when((x == 0) & jnp.logical_not(first))
    def _():
        greet(seq - jnp.where(head == 0, one, nil), (head + NH - 1) % NH)

    @pl.loop(0, HQ)
    def _(n):
        pltpu.make_async_copy(q_hbm.at[:, columns(n)], q_v.at[n], sems.at[0]).start()

    @pl.loop(0, 2 * HK)
    def _(n):
        pltpu.make_async_copy(kv_hbm.at[:, :, :, columns(n)], kcat.at[n, 1], sems.at[1]).start()

    base = (seq * NH + head) * 2
    vert = turned(vert_ref[...])
    slash = turned(slash_ref[...])
    fill_table(GQ, vert, turned(assign_ref[...]), table_v)
    to_smem = pltpu.make_async_copy(table_v, table, sems.at[14])
    to_smem.start()
    lane = lax.broadcasted_iota(jnp.int32, (HQ, 8 * BLK), 1) // BLK
    target = base + lane - 2
    listed = jnp.full((HQ, 8 * BLK), -1, jnp.int32)
    fresh = (target >= 0) & (lane < 4)
    for n in range(NV):
        col = vert[:, n : n + 1]
        listed = jnp.where(lane == 4 + n, col, listed)
        fresh = fresh & (target != col)
    for qb in range(2):
        off = qb + 2 - lane
        hit = (off >= 1) & ((slash[:, 0:1] == off) | (slash[:, 1:2] == off)) & fresh
        near = (lane < 4) & ((off == 0) | hit)
        far = (lane >= 4) & (listed >= 0) & (listed < base + qb)
        rows_bias[qb, :, 0] = jnp.where(near | far, 0.0, HIDE)
    row = lax.broadcasted_iota(jnp.int32, (ROWS, 2 * ROWS), 0)
    col = lax.broadcasted_iota(jnp.int32, (ROWS, 2 * ROWS), 1) - ROWS
    causal_bias[...] = jnp.where(col <= row, 0.0, HIDE)

    count = (NZ - 1) + (NY - 1) + (NX - 1) + 1
    count = count + jnp.where((x == NX - 1) & jnp.logical_not(last), one, nil)
    count = count + jnp.where(source, owners - own_source, nil)
    to_smem.wait()
    pl.semaphore_wait(barrier, count)

    def remote(src, dst, send, recv, to):
        return pltpu.make_async_remote_copy(
            src_ref=src,
            dst_ref=dst,
            send_sem=sems.at[send],
            recv_sem=sems.at[recv],
            device_id=to,
            device_id_type=MESH,
        )

    def entry(row, lane_, top):
        return jnp.minimum(jnp.maximum(table[row, lane_], 0), top)

    def await_bytes(ref, sem):
        pltpu.make_async_copy(ref, ref, sems.at[sem]).wait()

    @pl.when(source)
    def _():
        @pl.loop(0, owners)
        def _(o):
            core_, a_, c_ = o // (HK * NC), o // NC % HK, o % NC
            s_, h_ = device(core_, a_, home(a_, c_), c_)
            src = kv_hbm.at[:, c_, :, columns(2 * a_ + core_)]
            dst = tbuf.at[pl.ds(2 * head, 2)]
            mine = (s_ == seq) & (h_ == head)

            @pl.when(mine)
            def _():
                pltpu.make_async_copy(src, dst, sems.at[3]).start()

            @pl.when(jnp.logical_not(mine))
            def _():
                remote(src, dst, 2, 3, (s_, h_)).start()

    wrap = jnp.where(head == NH - 1, one, nil)

    @pl.when(jnp.logical_not(last))
    def _():
        @pl.loop(0, 2 * HK)
        def _(n):
            src = kv_hbm.at[:, :, :, columns(n)]
            remote(src, kcat.at[n, 0], 4, 5, (seq + wrap, (head + 1) % NH)).start()

    @pl.when(first)
    def _():
        kcat[:, 0] = jnp.zeros((2 * HK, *kcat.shape[2:]), kcat.dtype)

    for k in range(1, NX):
        pl.semaphore_signal(
            here_sem, inc=1, device_id=(seq, z * NX + (x + k) % NX), device_id_type=MESH
        )
    pl.semaphore_wait(here_sem, NX - 1)

    @pl.when(owner)
    def _():
        await_bytes(tbuf, 3)
        for r in range(VPOOL):
            piece[r] = tbuf[entry(a * GQ, 8 + r, 2 * NH - 1)]

        @pl.loop(0, NZ * NX)
        def _(k):
            b_, x_ = k // NX, k % NX
            mine = (b_ == b) & (x_ == x)
            dst = pool.at[core, a, :, x]

            @pl.when(mine)
            def _():
                pltpu.make_async_copy(piece, dst, sems.at[7]).start()

            @pl.when(jnp.logical_not(mine))
            def _():
                remote(piece, dst, 6, 7, device(core, a, b_, x_)).start()

    await_bytes(pool.at[core, a], 7)

    @pl.loop(1, NY)
    def _(k):
        remote(pool.at[core, a], pool.at[core, a], 8, 9, device(core, (a + k) % NY, b, x)).start()

    await_bytes(pool.at[core, pl.ds(0, NY - 1)], 9)
    swap = remote(pool.at[core], pool.at[core], 10, 11, (y * 2 + 1 - core, head))
    swap.start()
    await_bytes(q_v, 0)
    await_bytes(kcat.at[:, 1], 1)

    @pl.when(jnp.logical_not(first))
    def _():
        await_bytes(kcat.at[:, 0], 5)

    await_bytes(pool.at[1 - core], 11)

    factor = math.log2(math.e) / math.sqrt(HD)
    contract = (((1,), (1,)), ((), ()))

    def attend(d):
        c = entry(HQ + 2 * d, 5, HK - 1)
        keys = kcat[2 * c].reshape(2 * ROWS, HD)
        values = kcat[2 * c + 1].reshape(2 * ROWS, HD)
        heads = [entry(HQ + 2 * d + u, 4, HQ - 1) for u in range(2)]
        queries = [q_v[h] for h in heads]
        places = [
            [entry(HQ + 2 * d + u, n, VPOOL - 1) for n in range(NV)] for u in range(2)
        ]
        seen = lax.dot_general(
            jnp.concatenate(queries, axis=0), keys, contract, preferred_element_type=jnp.float32
        )
        nears, totals, numers = [], [], []
        for u in range(2):
            far_keys = jnp.concatenate([pool[0, c, p].reshape(BLK, HD) for p in places[u]], axis=0)
            far_values = jnp.concatenate(
                [pool[1, c, p].reshape(BLK, HD) for p in places[u]], axis=0
            )
            far = lax.dot_general(
                queries[u], far_keys, contract, preferred_element_type=jnp.float32
            )
            near = seen[u * ROWS : (u + 1) * ROWS] * factor + causal_bias[...]
            near = jnp.concatenate(
                [
                    near[qb * BLK : (qb + 1) * BLK] + rows_bias[qb, heads[u]][:, : 2 * ROWS]
                    for qb in range(2)
                ],
                axis=0,
            )
            far = far * factor
            far = jnp.concatenate(
                [
                    far[qb * BLK : (qb + 1) * BLK] + rows_bias[qb, heads[u]][:, 2 * ROWS :]
                    for qb in range(2)
                ],
                axis=0,
            )
            top = jnp.max(jnp.maximum(near, far), axis=1, keepdims=True)
            near = jnp.exp2(near - top)
            far = jnp.exp2(far - top)
            totals.append(jnp.sum(near + far, axis=1, keepdims=True))
            nears.append(near.astype(jnp.bfloat16))
            numers.append(
                jnp.dot(far.astype(jnp.bfloat16), far_values, preferred_element_type=jnp.float32)
            )
        joint = jnp.dot(
            jnp.concatenate(nears, axis=0), values, preferred_element_type=jnp.float32
        )
        for u in range(2):
            numer = joint[u * ROWS : (u + 1) * ROWS] + numers[u]
            stage[2 * d + u] = (numer / totals[u]).astype(jnp.bfloat16)

    here = pl.ds(pl.multiple_of(head * ROWS, ROWS), ROWS)

    @pl.loop(1, NH + 1)
    def _(k):
        d = (head + k) % NH
        attend(d)
        src = stage.at[pl.ds(2 * d, 2)]
        dst = out.at[:, here]

        @pl.when(k == NH)
        def _():
            pltpu.make_async_copy(src, dst, sems.at[13]).start()

        @pl.when(k < NH)
        def _():
            remote(src, dst, 12, 13, (seq, d)).start()

    await_bytes(out, 13)
    await_bytes(stage.at[pl.ds(0, 2 * NH - 2)], 12)
    await_bytes(pool.at[core], 10)
    await_bytes(pool.at[core, pl.ds(0, NY - 1)], 8)

    @pl.when(owner)
    def _():
        await_bytes(stage.at[pl.ds(0, NZ * NX - 1)], 6)

    @pl.when(jnp.logical_not(last))
    def _():
        await_bytes(kv_hbm, 4)

    @pl.when(source & owner)
    def _():
        await_bytes(stage.at[pl.ds(0, owners - 1), pl.ds(0, 32)], 2)

    @pl.when(source & jnp.logical_not(owner))
    def _():
        await_bytes(stage.at[pl.ds(0, owners), pl.ds(0, 32)], 2)


def on_device(sizes, queries, keys_values, vertical, slash, assignment):
    NS, NH, NZ, NY, HQ, HK = sizes
    width = keys_values.shape[1]
    vmem = pl.BlockSpec(memory_space=pltpu.VMEM)
    hbm = pl.BlockSpec(memory_space=pl.ANY)
    return pl.pallas_call(
        functools.partial(main_kernel, sizes),
        out_shape=jax.ShapeDtypeStruct((2, NH * ROWS, HD), jnp.bfloat16),
        in_specs=[vmem, vmem, vmem, hbm, hbm],
        out_specs=hbm,
        scratch_shapes=[
            pltpu.VMEM((HQ, ROWS, HD), jnp.bfloat16),
            pltpu.VMEM((2 * HK, 2, 2, NC, CH, HD), jnp.bfloat16),
            pltpu.VMEM((2 * NH, CH, HD), jnp.bfloat16),
            pltpu.VMEM((VPOOL, CH, HD), jnp.bfloat16),
            pltpu.VMEM((2, HK, VPOOL, NC, CH, HD), jnp.bfloat16),
            pltpu.VMEM((max(2 * NH, 2 * HK * NC), ROWS, HD), jnp.bfloat16),
            pltpu.VMEM((2, HQ, 1, 8 * BLK), jnp.float32),
            pltpu.VMEM((ROWS, 2 * ROWS), jnp.float32),
            pltpu.VMEM((2 * HQ, HD), jnp.int32),
            pltpu.SMEM((2 * HQ, HD), jnp.int32),
            pltpu.SemaphoreType.DMA((15,)),
            pltpu.SemaphoreType.REGULAR,
        ],
        compiler_params=pltpu.CompilerParams(
            collective_id=0, has_side_effects=True, vmem_limit_bytes=60 * 2**20
        ),
    )(
        vertical.T,
        slash.T,
        assignment.reshape(1, HQ),
        queries,
        keys_values.reshape(2, NC, CH, width),
    )


def solution(mesh):
    NS, NH = mesh.shape["seq"], mesh.shape["head"]
    sizes = (NS, NH, NH // NX, NS // 2, 2 * NH, NS // 2)
    placed = (P(("seq", "head"), None), P(("seq", "head"), None), P(), P(), P())
    return jax.shard_map(
        functools.partial(on_device, sizes),
        mesh=mesh,
        in_specs=placed,
        out_specs=P(("seq", "head"), None, None),
        check_vma=False,
    )
```

```python
import functools
import math

import jax
import jax.numpy as jnp
from jax import lax
from jax.experimental import pallas as pl
from jax.experimental.pallas import tpu as pltpu
from jax.sharding import PartitionSpec as P

HD = 128
BLK = 64
NV = 4
NX = 4
CH = 16
NC = BLK // CH
ROWS = 2 * BLK
VPOOL = 8
HIDE = -1e30
MESH = pl.DeviceIdType.MESH


def turned(rows):
    m = rows.shape[1]
    eye = (
        lax.broadcasted_iota(jnp.int32, (m, m), 0) == lax.broadcasted_iota(jnp.int32, (m, m), 1)
    ).astype(jnp.float32)
    return lax.dot_general(
        eye,
        rows.astype(jnp.float32),
        (((1,), (1,)), ((), ())),
        preferred_element_type=jnp.float32,
    ).astype(jnp.int32)


def fill_table(group, v, assign, out_ref):
    heads = v.shape[0]
    block = lax.broadcasted_iota(jnp.int32, (heads, BLK), 1)
    used = jnp.zeros((heads, BLK), jnp.float32)
    for n in range(NV):
        used = jnp.maximum(used, (v[:, n : n + 1] == block).astype(jnp.float32))
    one = lax.broadcasted_iota(jnp.int32, (heads, heads), 0)
    other = lax.broadcasted_iota(jnp.int32, (heads, heads), 1)
    same = (one // group == other // group).astype(jnp.float32)
    some = jnp.dot(same, used, preferred_element_type=jnp.float32)
    pool = (some > 0.5).astype(jnp.float32)
    before = (
        lax.broadcasted_iota(jnp.int32, (BLK, BLK), 0)
        < lax.broadcasted_iota(jnp.int32, (BLK, BLK), 1)
    ).astype(jnp.float32)
    rank = jnp.dot(pool, before, preferred_element_type=jnp.float32)
    lane = lax.broadcasted_iota(jnp.int32, (heads, HD), 1)
    table = jnp.zeros((heads, HD), jnp.float32)
    for n in range(NV):
        place = jnp.sum(jnp.where(v[:, n : n + 1] == block, rank, 0.0), axis=1, keepdims=True)
        table = jnp.where(lane == n, place, table)
    number = block.astype(jnp.float32)
    for r in range(VPOOL):
        held = (pool > 0.5) & (rank > r - 0.5) & (rank < r + 0.5)
        place = jnp.sum(jnp.where(held, number, 0.0), axis=1, keepdims=True)
        table = jnp.where(lane == 8 + r, place, table)
    head = lax.broadcasted_iota(jnp.int32, (heads, HD), 0)
    table = jnp.where(lane == 4, head.astype(jnp.float32), table)
    table = jnp.where(lane == 5, (head // group).astype(jnp.float32), table)
    chosen = (assign % heads == other).astype(jnp.float32)
    out_ref[:heads] = table.astype(jnp.int32)
    slots = jnp.dot(chosen, table, preferred_element_type=jnp.float32)
    out_ref[heads:] = slots.astype(jnp.int32)


def main_kernel(
    sizes,
    vert_ref,
    slash_ref,
    assign_ref,
    q_hbm,
    kv_hbm,
    out,
    q_v,
    kcat,
    tbuf,
    piece,
    pool,
    stage,
    rows_bias,
    causal_bias,
    table_v,
    table,
    sems,
    here_sem,
):
    NS, NH, NZ, NY, HQ, HK = sizes
    GQ = HQ // HK
    owners = 2 * HK * NC
    seq = lax.axis_index("seq")
    head = lax.axis_index("head")
    y, core = seq // 2, seq % 2
    z, x = head // NX, head % NX
    a = y + core * (z - y)
    b = z + core * (y - z)

    def device(core_, a_, b_, x_):
        y_ = a_ + core_ * (b_ - a_)
        z_ = b_ + core_ * (a_ - b_)
        return y_ * 2 + core_, z_ * NX + x_

    def home(a_, c_):
        return (a_ + 2 * c_) % NZ

    owner = b == home(a, x)
    source = seq == 0
    last = (seq == NS - 1) & (head == NH - 1)
    first = (seq == 0) & (head == 0)
    one = jnp.int32(1)
    nil = jnp.int32(0)
    own_source = jnp.where(owner & source, one, nil)

    def columns(n):
        return pl.ds(pl.multiple_of(n * HD, HD), HD)

    barrier = pltpu.get_barrier_semaphore()

    def greet(s_, h_):
        pl.semaphore_signal(barrier, inc=1, device_id=(s_, h_), device_id_type=MESH)

    @pl.when(owner)
    def _():
        @pl.loop(0, NH)
        def _(s):
            @pl.when(jnp.logical_not(source & (head == s)))
            def _():
                greet(0, s)

    @pl.loop(1, NZ)
    def _(k):
        greet(seq, (z + k) % NZ * NX + x)

    @pl.loop(1, NY)
    def _(k):
        greet((y + k) % NY * 2 + core, head)

    for k in range(1, NX):
        greet(seq, z * NX + (x + k) % NX)

    greet(y * 2 + 1 - core, head)

    @pl.when((x == 0) & jnp.logical_not(first))
    def _():
        greet(seq - jnp.where(head == 0, one, nil), (head + NH - 1) % NH)

    @pl.loop(0, HQ)
    def _(n):
        pltpu.make_async_copy(q_hbm.at[:, columns(n)], q_v.at[n], sems.at[0]).start()

    @pl.loop(0, 2 * HK)
    def _(n):
        pltpu.make_async_copy(kv_hbm.at[:, :, :, columns(n)], kcat.at[n, 1], sems.at[1]).start()

    base = (seq * NH + head) * 2
    vert = turned(vert_ref[...])
    slash = turned(slash_ref[...])
    fill_table(GQ, vert, turned(assign_ref[...]), table_v)
    to_smem = pltpu.make_async_copy(table_v, table, sems.at[14])
    to_smem.start()
    lane = lax.broadcasted_iota(jnp.int32, (HQ, 8 * BLK), 1) // BLK
    target = base + lane - 2
    listed = jnp.full((HQ, 8 * BLK), -1, jnp.int32)
    fresh = (target >= 0) & (lane < 4)
    for n in range(NV):
        col = vert[:, n : n + 1]
        listed = jnp.where(lane == 4 + n, col, listed)
        fresh = fresh & (target != col)
    for qb in range(2):
        off = qb + 2 - lane
        hit = (off >= 1) & ((slash[:, 0:1] == off) | (slash[:, 1:2] == off)) & fresh
        near = (lane < 4) & ((off == 0) | hit)
        far = (lane >= 4) & (listed >= 0) & (listed < base + qb)
        rows_bias[qb, :, 0] = jnp.where(near | far, 0.0, HIDE)
    row = lax.broadcasted_iota(jnp.int32, (ROWS, 2 * ROWS), 0)
    col = lax.broadcasted_iota(jnp.int32, (ROWS, 2 * ROWS), 1) - ROWS
    causal_bias[...] = jnp.where(col <= row, 0.0, HIDE)

    count = (NZ - 1) + (NY - 1) + (NX - 1) + 1
    count = count + jnp.where((x == NX - 1) & jnp.logical_not(last), one, nil)
    count = count + jnp.where(source, owners - own_source, nil)
    to_smem.wait()
    pl.semaphore_wait(barrier, count)

    def remote(src, dst, send, recv, to):
        return pltpu.make_async_remote_copy(
            src_ref=src,
            dst_ref=dst,
            send_sem=sems.at[send],
            recv_sem=sems.at[recv],
            device_id=to,
            device_id_type=MESH,
        )

    def entry(row, lane_, top):
        return jnp.minimum(jnp.maximum(table[row, lane_], 0), top)

    def far_first(place, k, size):
        return (place + size // 2 + (k + 1) // 2 * (1 - 2 * (k % 2)) + size) % size

    def await_bytes(ref, sem):
        pltpu.make_async_copy(ref, ref, sems.at[sem]).wait()

    @pl.when(source)
    def _():
        @pl.loop(0, owners)
        def _(o):
            core_, a_, c_ = o // (HK * NC), o // NC % HK, o % NC
            s_, h_ = device(core_, a_, home(a_, c_), c_)
            src = kv_hbm.at[:, c_, :, columns(2 * a_ + core_)]
            dst = tbuf.at[pl.ds(2 * head, 2)]
            mine = (s_ == seq) & (h_ == head)

            @pl.when(mine)
            def _():
                pltpu.make_async_copy(src, dst, sems.at[3]).start()

            @pl.when(jnp.logical_not(mine))
            def _():
                remote(src, dst, 2, 3, (s_, h_)).start()

    wrap = jnp.where(head == NH - 1, one, nil)

    @pl.when(jnp.logical_not(last))
    def _():
        @pl.loop(0, 2 * HK)
        def _(n):
            src = kv_hbm.at[:, :, :, columns(n)]
            remote(src, kcat.at[n, 0], 4, 5, (seq + wrap, (head + 1) % NH)).start()

    @pl.when(first)
    def _():
        kcat[:, 0] = jnp.zeros((2 * HK, *kcat.shape[2:]), kcat.dtype)

    for k in range(1, NX):
        pl.semaphore_signal(
            here_sem, inc=1, device_id=(seq, z * NX + (x + k) % NX), device_id_type=MESH
        )
    pl.semaphore_wait(here_sem, NX - 1)

    @pl.when(owner)
    def _():
        await_bytes(tbuf, 3)
        for r in range(VPOOL):
            piece[r] = tbuf[entry(a * GQ, 8 + r, 2 * NH - 1)]

        @pl.loop(0, NZ * NX)
        def _(k):
            b_, x_ = k // NX, k % NX
            mine = (b_ == b) & (x_ == x)
            dst = pool.at[core, a, :, x]

            @pl.when(mine)
            def _():
                pltpu.make_async_copy(piece, dst, sems.at[7]).start()

            @pl.when(jnp.logical_not(mine))
            def _():
                remote(piece, dst, 6, 7, device(core, a, b_, x_)).start()

    await_bytes(pool.at[core, a], 7)

    @pl.loop(0, NY - 1)
    def _(k):
        to = device(core, far_first(a, k, NY), b, x)
        remote(pool.at[core, a], pool.at[core, a], 8, 9, to).start()

    await_bytes(pool.at[core, pl.ds(0, NY - 1)], 9)
    swap = remote(pool.at[core], pool.at[core], 10, 11, (y * 2 + 1 - core, head))
    swap.start()
    await_bytes(q_v, 0)
    await_bytes(kcat.at[:, 1], 1)

    @pl.when(jnp.logical_not(first))
    def _():
        await_bytes(kcat.at[:, 0], 5)

    await_bytes(pool.at[1 - core], 11)

    factor = math.log2(math.e) / math.sqrt(HD)
    contract = (((1,), (1,)), ((), ()))

    def attend(d):
        c = entry(HQ + 2 * d, 5, HK - 1)
        keys = kcat[2 * c].reshape(2 * ROWS, HD)
        values = kcat[2 * c + 1].reshape(2 * ROWS, HD)
        heads = [entry(HQ + 2 * d + u, 4, HQ - 1) for u in range(2)]
        queries = [q_v[h] for h in heads]
        places = [
            [entry(HQ + 2 * d + u, n, VPOOL - 1) for n in range(NV)] for u in range(2)
        ]
        seen = lax.dot_general(
            jnp.concatenate(queries, axis=0), keys, contract, preferred_element_type=jnp.float32
        )
        nears, totals, numers = [], [], []
        for u in range(2):
            far_keys = jnp.concatenate([pool[0, c, p].reshape(BLK, HD) for p in places[u]], axis=0)
            far_values = jnp.concatenate(
                [pool[1, c, p].reshape(BLK, HD) for p in places[u]], axis=0
            )
            far = lax.dot_general(
                queries[u], far_keys, contract, preferred_element_type=jnp.float32
            )
            near = seen[u * ROWS : (u + 1) * ROWS] * factor + causal_bias[...]
            near = jnp.concatenate(
                [
                    near[qb * BLK : (qb + 1) * BLK] + rows_bias[qb, heads[u]][:, : 2 * ROWS]
                    for qb in range(2)
                ],
                axis=0,
            )
            far = far * factor
            far = jnp.concatenate(
                [
                    far[qb * BLK : (qb + 1) * BLK] + rows_bias[qb, heads[u]][:, 2 * ROWS :]
                    for qb in range(2)
                ],
                axis=0,
            )
            top = jnp.max(jnp.maximum(near, far), axis=1, keepdims=True)
            near = jnp.exp2(near - top)
            far = jnp.exp2(far - top)
            totals.append(jnp.sum(near + far, axis=1, keepdims=True))
            nears.append(near.astype(jnp.bfloat16))
            numers.append(
                jnp.dot(far.astype(jnp.bfloat16), far_values, preferred_element_type=jnp.float32)
            )
        joint = jnp.dot(
            jnp.concatenate(nears, axis=0), values, preferred_element_type=jnp.float32
        )
        for u in range(2):
            numer = joint[u * ROWS : (u + 1) * ROWS] + numers[u]
            stage[2 * d + u] = (numer / totals[u]).astype(jnp.bfloat16)

    here = pl.ds(pl.multiple_of(head * ROWS, ROWS), ROWS)

    @pl.loop(0, NH)
    def _(k):
        d = far_first(z, k // NX, NZ) * NX + (x + 1 + k) % NX
        attend(d)
        src = stage.at[pl.ds(2 * d, 2)]
        dst = out.at[:, here]

        @pl.when(k == NH - 1)
        def _():
            pltpu.make_async_copy(src, dst, sems.at[13]).start()

        @pl.when(k < NH - 1)
        def _():
            remote(src, dst, 12, 13, (seq, d)).start()

    await_bytes(out, 13)
    await_bytes(stage.at[pl.ds(0, 2 * NH - 2)], 12)
    await_bytes(pool.at[core], 10)
    await_bytes(pool.at[core, pl.ds(0, NY - 1)], 8)

    @pl.when(owner)
    def _():
        await_bytes(stage.at[pl.ds(0, NZ * NX - 1)], 6)

    @pl.when(jnp.logical_not(last))
    def _():
        await_bytes(kv_hbm, 4)

    @pl.when(source & owner)
    def _():
        await_bytes(stage.at[pl.ds(0, owners - 1), pl.ds(0, 32)], 2)

    @pl.when(source & jnp.logical_not(owner))
    def _():
        await_bytes(stage.at[pl.ds(0, owners), pl.ds(0, 32)], 2)


def on_device(sizes, queries, keys_values, vertical, slash, assignment):
    NS, NH, NZ, NY, HQ, HK = sizes
    width = keys_values.shape[1]
    vmem = pl.BlockSpec(memory_space=pltpu.VMEM)
    hbm = pl.BlockSpec(memory_space=pl.ANY)
    return pl.pallas_call(
        functools.partial(main_kernel, sizes),
        out_shape=jax.ShapeDtypeStruct((2, NH * ROWS, HD), jnp.bfloat16),
        in_specs=[vmem, vmem, vmem, hbm, hbm],
        out_specs=hbm,
        scratch_shapes=[
            pltpu.VMEM((HQ, ROWS, HD), jnp.bfloat16),
            pltpu.VMEM((2 * HK, 2, 2, NC, CH, HD), jnp.bfloat16),
            pltpu.VMEM((2 * NH, CH, HD), jnp.bfloat16),
            pltpu.VMEM((VPOOL, CH, HD), jnp.bfloat16),
            pltpu.VMEM((2, HK, VPOOL, NC, CH, HD), jnp.bfloat16),
            pltpu.VMEM((max(2 * NH, 2 * HK * NC), ROWS, HD), jnp.bfloat16),
            pltpu.VMEM((2, HQ, 1, 8 * BLK), jnp.float32),
            pltpu.VMEM((ROWS, 2 * ROWS), jnp.float32),
            pltpu.VMEM((2 * HQ, HD), jnp.int32),
            pltpu.SMEM((2 * HQ, HD), jnp.int32),
            pltpu.SemaphoreType.DMA((15,)),
            pltpu.SemaphoreType.REGULAR,
        ],
        compiler_params=pltpu.CompilerParams(
            collective_id=0, has_side_effects=True, vmem_limit_bytes=60 * 2**20
        ),
    )(
        vertical.T,
        slash.T,
        assignment.reshape(1, HQ),
        queries,
        keys_values.reshape(2, NC, CH, width),
    )


def solution(mesh):
    NS, NH = mesh.shape["seq"], mesh.shape["head"]
    sizes = (NS, NH, NH // NX, NS // 2, 2 * NH, NS // 2)
    placed = (P(("seq", "head"), None), P(("seq", "head"), None), P(), P(), P())
    return jax.shard_map(
        functools.partial(on_device, sizes),
        mesh=mesh,
        in_specs=placed,
        out_specs=P(("seq", "head"), None, None),
        check_vma=False,
    )
```

```python
import functools
import math

import jax
import jax.numpy as jnp
from jax import lax
from jax.experimental import pallas as pl
from jax.experimental.pallas import tpu as pltpu
from jax.sharding import PartitionSpec as P

HD = 128
BLK = 64
NV = 4
NX = 4
CH = 16
NC = BLK // CH
ROWS = 2 * BLK
VPOOL = 8
HIDE = -1e30
MESH = pl.DeviceIdType.MESH


def turned(rows):
    m = rows.shape[1]
    eye = (
        lax.broadcasted_iota(jnp.int32, (m, m), 0) == lax.broadcasted_iota(jnp.int32, (m, m), 1)
    ).astype(jnp.float32)
    return lax.dot_general(
        eye,
        rows.astype(jnp.float32),
        (((1,), (1,)), ((), ())),
        preferred_element_type=jnp.float32,
    ).astype(jnp.int32)


def fill_table(group, v, assign, out_ref):
    heads = v.shape[0]
    block = lax.broadcasted_iota(jnp.int32, (heads, BLK), 1)
    used = jnp.zeros((heads, BLK), jnp.float32)
    for n in range(NV):
        used = jnp.maximum(used, (v[:, n : n + 1] == block).astype(jnp.float32))
    one = lax.broadcasted_iota(jnp.int32, (heads, heads), 0)
    other = lax.broadcasted_iota(jnp.int32, (heads, heads), 1)
    same = (one // group == other // group).astype(jnp.float32)
    some = jnp.dot(same, used, preferred_element_type=jnp.float32)
    pool = (some > 0.5).astype(jnp.float32)
    before = (
        lax.broadcasted_iota(jnp.int32, (BLK, BLK), 0)
        < lax.broadcasted_iota(jnp.int32, (BLK, BLK), 1)
    ).astype(jnp.float32)
    rank = jnp.dot(pool, before, preferred_element_type=jnp.float32)
    lane = lax.broadcasted_iota(jnp.int32, (heads, HD), 1)
    table = jnp.zeros((heads, HD), jnp.float32)
    for n in range(NV):
        place = jnp.sum(jnp.where(v[:, n : n + 1] == block, rank, 0.0), axis=1, keepdims=True)
        table = jnp.where(lane == n, place, table)
    number = block.astype(jnp.float32)
    for r in range(VPOOL):
        held = (pool > 0.5) & (rank > r - 0.5) & (rank < r + 0.5)
        place = jnp.sum(jnp.where(held, number, 0.0), axis=1, keepdims=True)
        table = jnp.where(lane == 8 + r, place, table)
    head = lax.broadcasted_iota(jnp.int32, (heads, HD), 0)
    table = jnp.where(lane == 4, head.astype(jnp.float32), table)
    table = jnp.where(lane == 5, (head // group).astype(jnp.float32), table)
    chosen = (assign % heads == other).astype(jnp.float32)
    out_ref[:heads] = table.astype(jnp.int32)
    slots = jnp.dot(chosen, table, preferred_element_type=jnp.float32)
    out_ref[heads:] = slots.astype(jnp.int32)


def main_kernel(
    sizes,
    vert_ref,
    slash_ref,
    assign_ref,
    q_hbm,
    kv_hbm,
    out,
    q_v,
    kcat,
    tbuf,
    piece,
    pool,
    stage,
    rows_bias,
    causal_bias,
    table_v,
    table,
    sems,
    here_sem,
):
    NS, NH, NZ, NY, HQ, HK = sizes
    GQ = HQ // HK
    owners = 2 * HK * NC
    seq = lax.axis_index("seq")
    head = lax.axis_index("head")
    y, core = seq // 2, seq % 2
    z, x = head // NX, head % NX
    a = y + core * (z - y)
    b = z + core * (y - z)

    def device(core_, a_, b_, x_):
        y_ = a_ + core_ * (b_ - a_)
        z_ = b_ + core_ * (a_ - b_)
        return y_ * 2 + core_, z_ * NX + x_

    def home(a_, c_):
        return (a_ + 2 * c_) % NZ

    owner = b == home(a, x)
    source = seq == 0
    last = (seq == NS - 1) & (head == NH - 1)
    first = (seq == 0) & (head == 0)
    one = jnp.int32(1)
    nil = jnp.int32(0)
    own_source = jnp.where(owner & source, one, nil)

    def columns(n):
        return pl.ds(pl.multiple_of(n * HD, HD), HD)

    barrier = pltpu.get_barrier_semaphore()

    def greet(s_, h_):
        pl.semaphore_signal(barrier, inc=1, device_id=(s_, h_), device_id_type=MESH)

    @pl.loop(1, NZ)
    def _(k):
        greet(seq, (z + k) % NZ * NX + x)

    @pl.loop(1, NY)
    def _(k):
        greet((y + k) % NY * 2 + core, head)

    for k in range(1, NX):
        greet(seq, z * NX + (x + k) % NX)

    greet(y * 2 + 1 - core, head)

    @pl.when((x == 0) & jnp.logical_not(first))
    def _():
        greet(seq - jnp.where(head == 0, one, nil), (head + NH - 1) % NH)

    @pl.when(owner)
    def _():
        @pl.loop(0, NH)
        def _(s):
            @pl.when(jnp.logical_not(source & (head == s)))
            def _():
                greet(0, s)

    @pl.loop(0, HQ)
    def _(n):
        pltpu.make_async_copy(q_hbm.at[:, columns(n)], q_v.at[n], sems.at[0]).start()

    @pl.loop(0, 2 * HK)
    def _(n):
        pltpu.make_async_copy(kv_hbm.at[:, :, :, columns(n)], kcat.at[n, 1], sems.at[1]).start()

    base = (seq * NH + head) * 2
    vert = turned(vert_ref[...])
    slash = turned(slash_ref[...])
    fill_table(GQ, vert, turned(assign_ref[...]), table_v)
    to_smem = pltpu.make_async_copy(table_v, table, sems.at[14])
    to_smem.start()
    lane = lax.broadcasted_iota(jnp.int32, (HQ, 8 * BLK), 1) // BLK
    target = base + lane - 2
    listed = jnp.full((HQ, 8 * BLK), -1, jnp.int32)
    fresh = (target >= 0) & (lane < 4)
    for n in range(NV):
        col = vert[:, n : n + 1]
        listed = jnp.where(lane == 4 + n, col, listed)
        fresh = fresh & (target != col)
    for qb in range(2):
        off = qb + 2 - lane
        hit = (off >= 1) & ((slash[:, 0:1] == off) | (slash[:, 1:2] == off)) & fresh
        near = (lane < 4) & ((off == 0) | hit)
        far = (lane >= 4) & (listed >= 0) & (listed < base + qb)
        rows_bias[qb, :, 0] = jnp.where(near | far, 0.0, HIDE)
    row = lax.broadcasted_iota(jnp.int32, (ROWS, 2 * ROWS), 0)
    col = lax.broadcasted_iota(jnp.int32, (ROWS, 2 * ROWS), 1) - ROWS
    causal_bias[...] = jnp.where(col <= row, 0.0, HIDE)

    count = (NZ - 1) + (NY - 1) + (NX - 1) + 1
    count = count + jnp.where((x == NX - 1) & jnp.logical_not(last), one, nil)
    count = count + jnp.where(source, owners - own_source, nil)
    to_smem.wait()
    pl.semaphore_wait(barrier, count)

    def remote(src, dst, send, recv, to):
        return pltpu.make_async_remote_copy(
            src_ref=src,
            dst_ref=dst,
            send_sem=sems.at[send],
            recv_sem=sems.at[recv],
            device_id=to,
            device_id_type=MESH,
        )

    def entry(row, lane_, top):
        return jnp.minimum(jnp.maximum(table[row, lane_], 0), top)

    def far_first(place, k, size):
        return (place + size // 2 + (k + 1) // 2 * (1 - 2 * (k % 2)) + size) % size

    def await_bytes(ref, sem):
        pltpu.make_async_copy(ref, ref, sems.at[sem]).wait()

    @pl.when(source)
    def _():
        @pl.loop(0, owners)
        def _(o):
            core_, a_, c_ = o // (HK * NC), o % HK, o // HK % NC
            s_, h_ = device(core_, a_, home(a_, c_), c_)
            src = kv_hbm.at[:, c_, :, columns(2 * a_ + core_)]
            dst = tbuf.at[pl.ds(2 * head, 2)]
            mine = (s_ == seq) & (h_ == head)

            @pl.when(mine)
            def _():
                pltpu.make_async_copy(src, dst, sems.at[3]).start()

            @pl.when(jnp.logical_not(mine))
            def _():
                remote(src, dst, 2, 3, (s_, h_)).start()

    wrap = jnp.where(head == NH - 1, one, nil)

    @pl.when(first)
    def _():
        kcat[:, 0] = jnp.zeros((2 * HK, *kcat.shape[2:]), kcat.dtype)

    for k in range(1, NX):
        pl.semaphore_signal(
            here_sem, inc=1, device_id=(seq, z * NX + (x + k) % NX), device_id_type=MESH
        )
    pl.semaphore_wait(here_sem, NX - 1)

    @pl.when(owner)
    def _():
        await_bytes(tbuf, 3)
        for r in range(VPOOL):
            piece[r] = tbuf[entry(a * GQ, 8 + r, 2 * NH - 1)]

        @pl.loop(0, NZ * NX)
        def _(k):
            b_, x_ = k // NX, k % NX
            mine = (b_ == b) & (x_ == x)
            dst = pool.at[core, a, :, x]

            @pl.when(mine)
            def _():
                pltpu.make_async_copy(piece, dst, sems.at[7]).start()

            @pl.when(jnp.logical_not(mine))
            def _():
                remote(piece, dst, 6, 7, device(core, a, b_, x_)).start()

    @pl.when(jnp.logical_not(last))
    def _():
        @pl.loop(0, 2 * HK)
        def _(n):
            src = kv_hbm.at[:, :, :, columns(n)]
            remote(src, kcat.at[n, 0], 4, 5, (seq + wrap, (head + 1) % NH)).start()

    await_bytes(pool.at[core, a], 7)

    @pl.loop(0, NY - 1)
    def _(k):
        to = device(core, far_first(a, k, NY), b, x)
        remote(pool.at[core, a], pool.at[core, a], 8, 15 + a, to).start()

    @pl.loop(0, HK)
    def _(k):
        a_ = far_first(a, HK - 1 - k, HK)

        @pl.when(k > 0)
        def _():
            await_bytes(pool.at[core, a_], 15 + a_)

        remote(pool.at[core, a_], pool.at[core, a_], 10, 11, (y * 2 + 1 - core, head)).start()

    await_bytes(q_v, 0)
    await_bytes(kcat.at[:, 1], 1)

    @pl.when(jnp.logical_not(first))
    def _():
        await_bytes(kcat.at[:, 0], 5)

    await_bytes(pool.at[1 - core], 11)

    factor = math.log2(math.e) / math.sqrt(HD)
    contract = (((1,), (1,)), ((), ()))

    def attend(d):
        c = entry(HQ + 2 * d, 5, HK - 1)
        keys = kcat[2 * c].reshape(2 * ROWS, HD)
        values = kcat[2 * c + 1].reshape(2 * ROWS, HD)
        heads = [entry(HQ + 2 * d + u, 4, HQ - 1) for u in range(2)]
        queries = [q_v[h] for h in heads]
        places = [
            [entry(HQ + 2 * d + u, n, VPOOL - 1) for n in range(NV)] for u in range(2)
        ]
        seen = lax.dot_general(
            jnp.concatenate(queries, axis=0), keys, contract, preferred_element_type=jnp.float32
        )
        nears, totals, numers = [], [], []
        for u in range(2):
            far_keys = jnp.concatenate([pool[0, c, p].reshape(BLK, HD) for p in places[u]], axis=0)
            far_values = jnp.concatenate(
                [pool[1, c, p].reshape(BLK, HD) for p in places[u]], axis=0
            )
            far = lax.dot_general(
                queries[u], far_keys, contract, preferred_element_type=jnp.float32
            )
            near = seen[u * ROWS : (u + 1) * ROWS] * factor + causal_bias[...]
            near = jnp.concatenate(
                [
                    near[qb * BLK : (qb + 1) * BLK] + rows_bias[qb, heads[u]][:, : 2 * ROWS]
                    for qb in range(2)
                ],
                axis=0,
            )
            far = far * factor
            far = jnp.concatenate(
                [
                    far[qb * BLK : (qb + 1) * BLK] + rows_bias[qb, heads[u]][:, 2 * ROWS :]
                    for qb in range(2)
                ],
                axis=0,
            )
            top = jnp.max(jnp.maximum(near, far), axis=1, keepdims=True)
            near = jnp.exp2(near - top)
            far = jnp.exp2(far - top)
            totals.append(jnp.sum(near + far, axis=1, keepdims=True))
            nears.append(near.astype(jnp.bfloat16))
            numers.append(
                jnp.dot(far.astype(jnp.bfloat16), far_values, preferred_element_type=jnp.float32)
            )
        joint = jnp.dot(
            jnp.concatenate(nears, axis=0), values, preferred_element_type=jnp.float32
        )
        for u in range(2):
            numer = joint[u * ROWS : (u + 1) * ROWS] + numers[u]
            stage[2 * d + u] = (numer / totals[u]).astype(jnp.bfloat16)

    here = pl.ds(pl.multiple_of(head * ROWS, ROWS), ROWS)

    @pl.loop(0, NH)
    def _(k):
        d = far_first(z, k // NX, NZ) * NX + (x + 1 + k) % NX
        attend(d)
        src = stage.at[pl.ds(2 * d, 2)]
        dst = out.at[:, here]

        @pl.when(k == NH - 1)
        def _():
            pltpu.make_async_copy(src, dst, sems.at[13]).start()

        @pl.when(k < NH - 1)
        def _():
            remote(src, dst, 12, 13, (seq, d)).start()

    await_bytes(out, 13)
    await_bytes(stage.at[pl.ds(0, 2 * NH - 2)], 12)
    await_bytes(pool.at[core], 10)
    await_bytes(pool.at[core, pl.ds(0, NY - 1)], 8)

    @pl.when(owner)
    def _():
        await_bytes(stage.at[pl.ds(0, NZ * NX - 1)], 6)

    @pl.when(jnp.logical_not(last))
    def _():
        await_bytes(kv_hbm, 4)

    @pl.when(source & owner)
    def _():
        await_bytes(stage.at[pl.ds(0, owners - 1), pl.ds(0, 32)], 2)

    @pl.when(source & jnp.logical_not(owner))
    def _():
        await_bytes(stage.at[pl.ds(0, owners), pl.ds(0, 32)], 2)


def on_device(sizes, queries, keys_values, vertical, slash, assignment):
    NS, NH, NZ, NY, HQ, HK = sizes
    width = keys_values.shape[1]
    vmem = pl.BlockSpec(memory_space=pltpu.VMEM)
    hbm = pl.BlockSpec(memory_space=pl.ANY)
    return pl.pallas_call(
        functools.partial(main_kernel, sizes),
        out_shape=jax.ShapeDtypeStruct((2, NH * ROWS, HD), jnp.bfloat16),
        in_specs=[vmem, vmem, vmem, hbm, hbm],
        out_specs=hbm,
        scratch_shapes=[
            pltpu.VMEM((HQ, ROWS, HD), jnp.bfloat16),
            pltpu.VMEM((2 * HK, 2, 2, NC, CH, HD), jnp.bfloat16),
            pltpu.VMEM((2 * NH, CH, HD), jnp.bfloat16),
            pltpu.VMEM((VPOOL, CH, HD), jnp.bfloat16),
            pltpu.VMEM((2, HK, VPOOL, NC, CH, HD), jnp.bfloat16),
            pltpu.VMEM((max(2 * NH, 2 * HK * NC), ROWS, HD), jnp.bfloat16),
            pltpu.VMEM((2, HQ, 1, 8 * BLK), jnp.float32),
            pltpu.VMEM((ROWS, 2 * ROWS), jnp.float32),
            pltpu.VMEM((2 * HQ, HD), jnp.int32),
            pltpu.SMEM((2 * HQ, HD), jnp.int32),
            pltpu.SemaphoreType.DMA((15 + HK,)),
            pltpu.SemaphoreType.REGULAR,
        ],
        compiler_params=pltpu.CompilerParams(
            collective_id=0, has_side_effects=True, vmem_limit_bytes=60 * 2**20
        ),
    )(
        vertical.T,
        slash.T,
        assignment.reshape(1, HQ),
        queries,
        keys_values.reshape(2, NC, CH, width),
    )


def solution(mesh):
    NS, NH = mesh.shape["seq"], mesh.shape["head"]
    sizes = (NS, NH, NH // NX, NS // 2, 2 * NH, NS // 2)
    placed = (P(("seq", "head"), None), P(("seq", "head"), None), P(), P(), P())
    return jax.shard_map(
        functools.partial(on_device, sizes),
        mesh=mesh,
        in_specs=placed,
        out_specs=P(("seq", "head"), None, None),
        check_vma=False,
    )
```
